32 devices in a mesh: groups: 2 (over x), blk: 8 (over z, y), inner: 2 (over core).
Axes of the slice: x: 2, y: 2, z: 4, core: 2. Of those that a mesh axis runs over, the one named last changes fastest.
Arguments:
- embeddings: bfloat16 [16384, 1024], P(('groups', 'blk', 'inner')), parts along dimension 0, may hold values from -30 to 30
- cluster_ids: int32 [16384], P(('groups', 'blk', 'inner')), parts along dimension 0, may hold values from 0 to 15
- live_rows: int32 [32], P(('groups', 'blk', 'inner')), parts along dimension 0, may hold values from 1 to 512, 6144 in all
Outputs:
- weights: float32 [16384], P(('groups', 'blk', 'inner')), parts along dimension 0
The draws below stay inside these ranges and needn't reach their ends.
There are 2 independent parts, one for each index of `groups`. The reference program is written for one: setup_inputs(seed, part) draws one part's arguments, and reference() takes and returns one part's arrays. A program takes and returns all parts, laid end to end along the dimension named above; each array names one. Nothing has to cross between parts.
Inputs may be any that keep to these rules, and one draw needn't show every extreme that they name: `live_rows`: some shard is full.
All inputs are finite; a program needn't handle non-finite values.
Results may differ from the reference program's by a relative error of at most 0.0047.
Values may be sent and summed in bfloat16 or wider, within the bound.
A program may use at most 64 MiB of HBM per device.

```python
import math
import jax
import jax.numpy as jnp
import numpy as np
from jax import lax

D = 1024
ROW_DEV = 512
CLUSTERS = 16
SHARDS = 16
ROWS = 8192
LIVE_TOTAL = 6144


def draw_embeddings(key, part):
    key = jax.random.fold_in(key, 11)
    subkeys = jax.random.split(key, 4)
    prototypes = jax.random.normal(subkeys[0], (64, D), jnp.float32)
    proto_pick = jax.random.randint(subkeys[1], (ROWS,), 0, 64)
    strength = jax.random.uniform(subkeys[2], (ROWS, 1), jnp.float32, 0.3, 2.5)
    noise_part = jax.random.normal(subkeys[3], (ROWS, D), jnp.float32)
    return jnp.clip(strength * prototypes[proto_pick] + noise_part, -30.0, 30.0).astype(jnp.bfloat16)


def with_ends(drawn, rng, low, largest):
    longest = drawn.shape.index(max(drawn.shape))
    spots = []
    for shift in (0, 1):
        where = [jax.random.randint(jax.random.fold_in(rng, axis), (), 0, length) for axis, length in enumerate(drawn.shape)]
        where[longest] = (where[longest] + shift) % drawn.shape[longest]
        spots.append(tuple(where))
    return drawn.at[spots[0]].set(low).at[spots[1]].set(largest)


def length_profile(number_of, total, reach, slope):
    portions = [(1 << 20) // math.isqrt(grade ** slope) + 1 for grade in range(2, number_of + 1)]
    spare, holding = total - reach - (number_of - 1), [1] * (number_of - 1)
    while spare > 0:
        movable = [i for i in range(number_of - 1) if holding[i] < reach]
        pool, budget = sum([portions[i] for i in movable]), spare
        for i in movable:
            extra = min(reach - holding[i], max(1, budget * portions[i] // pool), spare)
            holding[i] = holding[i] + extra
            spare = spare - extra
    return np.array([reach] + holding)


def uneven(stream_key, amount, total, reach, lean):
    if amount == 2:
        one = jax.random.randint(stream_key, (), max(1, total - reach), min(reach, total - 1) + 1)
        return jnp.stack([one, total - one])
    tallies = jnp.asarray(length_profile(amount, total, reach, lean), jnp.int32)
    couples = (amount - 1) // 2
    source_of, sink = tallies[1:1 + 2 * couples:2], tallies[2:2 + 2 * couples:2]
    slack = jnp.minimum(source_of - 1, reach - sink)
    moved = jax.random.randint(jax.random.fold_in(stream_key, 1), (couples,), 0, 1 << 20) % (slack + 1)
    tallies = tallies.at[1:1 + 2 * couples:2].set(source_of - moved).at[2:2 + 2 * couples:2].set(sink + moved)
    return tallies[jax.random.permutation(jax.random.fold_in(stream_key, 2), amount)]


def setup_inputs(seed: int = 0, part: int = 0) -> dict:
    streams_of = jax.random.split(jax.random.key(seed), 4)
    part_keys = jax.random.split(jax.random.fold_in(streams_of[3], part), 4)
    embeddings = draw_embeddings(jax.random.fold_in(jax.random.fold_in(streams_of[3], part), 71), part)
    cluster_ids = with_ends(jax.random.randint(part_keys[1], (ROWS,), 0, CLUSTERS), jax.random.fold_in(part_keys[1], 1), 0, CLUSTERS - 1).astype(jnp.int32)
    live_rows = uneven(part_keys[2], SHARDS, LIVE_TOTAL, ROW_DEV, 2).astype(jnp.int32)
    return {"embeddings": embeddings, "cluster_ids": cluster_ids, "live_rows": live_rows}


sharpness = 8.0
cross_weight = 0.25
base_weight = 8.0
epsilon = 1e-06

def reference(embeddings, cluster_ids, live_rows):
    widened = embeddings.astype(jnp.float32)
    scaled = lax.rsqrt(lax.optimization_barrier(jnp.mean(widened * widened, axis=1, keepdims=True)) + epsilon) / math.sqrt(D)
    unit_rows = (widened * scaled).astype(jnp.bfloat16)
    position = jnp.arange(ROWS, dtype=jnp.int32)
    alive = position % ROW_DEV < live_rows[position // ROW_DEV]
    row_tags = jnp.where(alive, cluster_ids, -1)
    row_mask = (row_tags >= 0).astype(jnp.float32)

    def score_block(pieces):
        unit_block, tag_block, mask_block = pieces
        cosines = jnp.dot(unit_block, unit_rows.T, preferred_element_type=jnp.float32)
        weighting = jnp.where(tag_block[:, None] == row_tags[None, :], 1.0, cross_weight)
        weighting = weighting * mask_block[:, None] * row_mask[None, :]
        return lax.optimization_barrier(jnp.sum(jnp.exp(sharpness * (cosines - 1.0)) * weighting, axis=1))
    density = lax.map(score_block, (unit_rows.reshape(SHARDS, ROW_DEV, D), row_tags.reshape(SHARDS, ROW_DEV), row_mask.reshape(SHARDS, ROW_DEV))).reshape(ROWS)
    return row_mask * base_weight / (density + 1.0 - row_mask)
```

```python
import functools
import math

import jax
import jax.numpy as jnp
from jax import lax
from jax.experimental import pallas as pl
from jax.experimental.pallas import tpu as pltpu
from jax.sharding import PartitionSpec as P

sharpness = 8.0
epsilon = 1e-06
base_weight = 8.0
MESH = pl.DeviceIdType.MESH
LOG2E = 1.4426950408889634
COLS = 2
QUAD = 2 * COLS
NEG = -1e30


def kernel(
    stages, chunks, emb, ids, live, out,
    quad, vis, tags, tag_col, cap_col, acc, vsum, rsum, gpart, gsum,
    fwd_send, own_send, vis_recv, y_send, y_recv, i_send, i_recv, d_send, d_recv,
    t_send, t_recv, r_send, r_recv, g_send, g_recv,
):
    rows, depth = emb.shape
    span = rows // chunks
    half = stages // 2 - 1
    blk, core = lax.axis_index("blk"), lax.axis_index("inner")
    stage, col = blk // COLS, blk % COLS
    upper = stage // (half + 1)
    q = col * 2 + core
    me = blk * 2 + core
    peers = stages * QUAD

    def at(s, y, c):
        return {"blk": s * COLS + y, "inner": c}

    def peer_of(index):
        return {"blk": index // 2, "inner": index % 2}

    def part(k):
        return pl.ds(pl.multiple_of(k * span, span), span)

    def remote(src, dst, send, recv, device):
        return pltpu.make_async_remote_copy(
            src_ref=src, dst_ref=dst, send_sem=send, recv_sem=recv,
            device_id=device, device_id_type=MESH,
        )

    def own_forward(k):
        return remote(quad.at[q, part(k)], vis.at[0, part(k)], own_send.at[k], vis_recv.at[0, k],
                      at(stage + 1, col, core))

    def own_back(k):
        return remote(quad.at[q, part(k)], vis.at[half + 1, part(k)], own_send.at[k],
                      vis_recv.at[half + 1, k], at(stage - 1, col, core))

    def pass_forward(s, k):
        slot = s + 1 - upper
        return remote(vis.at[s, part(k)], vis.at[slot, part(k)], fwd_send.at[s, k],
                      vis_recv.at[slot, k], at(stage + 1, col, core))

    def pass_back(s, k):
        slot = half + 1 + s
        return remote(vis.at[slot, part(k)], vis.at[slot + 1, part(k)], fwd_send.at[slot, k],
                      vis_recv.at[slot + 1, k], at(stage - 1, col, core))

    def arrival(slot, k):
        return remote(vis.at[slot, part(k)], vis.at[slot, part(k)], fwd_send.at[slot, k],
                      vis_recv.at[slot, k], at(stage, col, 1 - core))

    def across(owner, k):
        return remote(quad.at[owner, part(k)], quad.at[owner, part(k)], y_send.at[k], y_recv.at[k],
                      at(stage, 1 - col, core))

    def beside(owner, k):
        return remote(quad.at[owner, part(k)], quad.at[owner, part(k)], i_send.at[k], i_recv.at[k],
                      at(stage, col, 1 - core))

    def diagonal(owner, k):
        return remote(quad.at[owner, part(k)], quad.at[owner, part(k)], d_send.at[k], d_recv.at[k],
                      at(stage, col, 1 - core))

    def tag_copy(owner, sem, device):
        return remote(tags.at[owner], tags.at[owner], t_send.at[sem], t_recv.at[owner], device)

    q_across, q_beside = (1 - col) * 2 + core, col * 2 + 1 - core
    q_diag = (1 - col) * 2 + 1 - core

    barrier = pltpu.get_barrier_semaphore()

    def greet(p, _):
        pl.semaphore_signal(barrier, inc=1, device_id=peer_of((me + p) % peers), device_id_type=MESH)
        return 0

    lax.fori_loop(1, peers, greet, 0)

    def normalize(k):
        wide = emb[part(k), :].astype(jnp.float32)
        scale = lax.rsqrt(jnp.mean(wide * wide, axis=1, keepdims=True) + epsilon) / math.sqrt(depth)
        quad[q, part(k), :] = (wide * scale).astype(jnp.bfloat16)

    position = lax.broadcasted_iota(jnp.int32, (1, rows), 1)
    tags[me] = jnp.where(position < live[0], ids[...], -1).astype(jnp.float32)
    normalize(0)
    pl.semaphore_wait(barrier, peers - 1)

    def start_own(k):
        @pl.when(stage <= half)
        def _():
            own_forward(k).start()

        @pl.when(stage >= half + 2)
        def _():
            own_back(k).start()

        across(q, k).start()
        beside(q, k).start()

    def send_tags(p, _):
        tag_copy(me, p, peer_of((me + p) % peers)).start()
        return 0

    start_own(0)
    lax.fori_loop(1, peers, send_tags, 0)

    def rest(k, _):
        normalize(k)
        start_own(k)
        return 0

    lax.fori_loop(1, chunks, rest, 0)

    def receive(s, k):
        @pl.when(stage > s)
        def _():
            arrival(s, k).wait_recv()

            @pl.when(stage < stages - 1)
            def _():
                pass_forward(s, k).start()

        if s <= stages - 3 - half:
            @pl.when((stage > half) & (stage + s < stages - 1))
            def _():
                arrival(half + 1 + s, k).wait_recv()

                @pl.when(stage >= half + 2)
                def _():
                    pass_back(s, k).start()

    def first(k, _):
        receive(0, k)
        across(q_across, k).wait_recv()
        diagonal(q_across, k).start()
        return 0

    lax.fori_loop(0, chunks, first, 0)

    def take_tags(p, _):
        tag_copy((me + p) % peers, p, peer_of((me + p) % peers)).wait_recv()
        return 0

    lax.fori_loop(1, peers, take_tags, 0)
    for g in range(QUAD):
        row = tags[stage * QUAD + g]
        tall = jnp.broadcast_to(row, (128, rows)).T
        tag_col[g] = tall
        cap_col[g] = jnp.where(tall < 0, NEG, 0.0)
        acc[g] = jnp.zeros((rows, 128), jnp.float32)

    def settle(k, _):
        beside(q_beside, k).wait_recv()
        diagonal(q_diag, k).wait_recv()
        return 0

    lax.fori_loop(0, chunks, settle, 0)

    def visit(block, owner, slot, k, keep):
        seen = block[part(k), :]
        lanes = pl.ds(pl.multiple_of(k * span, span), span)
        tag_row = tags[owner, :, lanes]
        same = jnp.where(tag_row < 0, NEG, -sharpness * LOG2E)
        other = same - 2.0

        def tile(g, total):
            cosines = lax.dot_general(
                quad[g], seen, (((1,), (1,)), ((), ())), preferred_element_type=jnp.float32
            )
            bias = jnp.where(tag_col[g] == tag_row, same, other) + cap_col[g]
            weight = jnp.exp2(cosines * (sharpness * LOG2E) + bias)
            if keep:
                acc[g] += weight
            return total + jnp.sum(weight.reshape(rows // 8, 8, span), axis=0)

        total = lax.fori_loop(0, QUAD, tile, jnp.zeros((8, span), jnp.float32))
        vsum[slot, :, lanes] = jnp.sum(total, axis=0, keepdims=True)

    def owner_of(visitor):
        return visitor * QUAD + q

    def visit_forward(s, k):
        @pl.when((stage > s) & (stage <= half))
        def _():
            visit(vis.at[s], owner_of(stage - 1 - s), s, k, True)

        @pl.when(stage > half)
        def _():
            visit(vis.at[s], owner_of(half - s), s, k, True)

    def visit_back(s, k):
        if s <= stages - 3 - half:
            @pl.when((stage > half) & (stage + s < stages - 1))
            def _():
                visit(vis.at[half + 1 + s], owner_of(stage + 1 + s), half + 1 + s, k, True)

    for s in range(1, half + 1):
        def turn(k, _):
            if s == 1:
                visit(quad.at[q], me, stages - 1, k, False)
                visit_forward(0, k)
                visit_back(0, k)
            receive(s, k)
            visit_forward(s, k)
            visit_back(s, k)
            return 0

        lax.fori_loop(0, chunks, turn, 0)

    def give_back(slot, visitor):
        return remote(vsum.at[slot], rsum.at[stage], r_send.at[slot], r_recv.at[stage],
                      at(visitor, col, core))

    def each_return(act):
        for s in range(half + 1):
            @pl.when((stage > s) & (stage <= half))
            def _():
                act(give_back(s, stage - 1 - s))

            @pl.when(stage > half)
            def _():
                act(give_back(s, half - s))

            if s <= stages - 3 - half:
                @pl.when((stage > half) & (stage + s < stages - 1))
                def _():
                    act(give_back(half + 1 + s, stage + 1 + s))

    each_return(lambda copy: copy.start())
    for g in range(QUAD):
        gpart[g] = jnp.sum(acc[g].T, axis=0, keepdims=True)

    def share(step):
        g = (q + step) % QUAD
        return remote(gpart.at[g], gsum.at[q], g_send.at[step], g_recv.at[q], at(stage, g // 2, g % 2))

    def shared(step):
        g = (q + step) % QUAD
        return remote(gpart.at[g], gsum.at[g], g_send.at[step], g_recv.at[g], at(stage, g // 2, g % 2))

    for step in range(1, QUAD):
        share(step).start()
    vsum[stages - 1] = vsum[stages - 1] + gpart[q]
    for other in range(stages):
        @pl.when(((stage <= half) & (other > stage)) | ((stage > other) & (other > half)))
        def _():
            remote(rsum.at[other], rsum.at[other], r_send.at[0], r_recv.at[other],
                   at(stage, col, 1 - core)).wait_recv()
            vsum[stages - 1] = vsum[stages - 1] + rsum[other]

    for step in range(1, QUAD):
        shared(step).wait_recv()
        vsum[stages - 1] = vsum[stages - 1] + gsum[(q + step) % QUAD]
    mask = (tags[me] >= 0).astype(jnp.float32)
    out[...] = mask * base_weight / (vsum[stages - 1] + 1.0 - mask)

    def drain(k, _):
        @pl.when(stage <= half)
        def _():
            own_forward(k).wait_send()

        @pl.when(stage >= half + 2)
        def _():
            own_back(k).wait_send()

        across(q, k).wait_send()
        beside(q, k).wait_send()
        diagonal(q_across, k).wait_send()
        for s in range(half + 1):
            @pl.when((stage > s) & (stage < stages - 1))
            def _():
                pass_forward(s, k).wait_send()

            if s <= stages - 3 - half:
                @pl.when((stage >= half + 2) & (stage + s < stages - 1))
                def _():
                    pass_back(s, k).wait_send()
        return 0

    lax.fori_loop(0, chunks, drain, 0)

    def drain_tags(p, _):
        tag_copy(me, p, peer_of((me + p) % peers)).wait_send()
        return 0

    lax.fori_loop(1, peers, drain_tags, 0)
    each_return(lambda copy: copy.wait_send())
    for step in range(1, QUAD):
        share(step).wait_send()


def solution(mesh):
    stages = mesh.shape["blk"] // COLS

    def body(embeddings, cluster_ids, live_rows):
        rows, depth = embeddings.shape
        chunks = 4
        peers = stages * QUAD
        dma = pltpu.SemaphoreType.DMA
        f32 = jnp.float32
        weights = pl.pallas_call(
            functools.partial(kernel, stages, chunks),
            out_shape=jax.ShapeDtypeStruct((1, rows), f32),
            in_specs=[
                pl.BlockSpec(memory_space=pltpu.VMEM),
                pl.BlockSpec(memory_space=pltpu.VMEM),
                pl.BlockSpec(memory_space=pltpu.SMEM),
            ],
            out_specs=pl.BlockSpec(memory_space=pltpu.VMEM),
            scratch_shapes=[
                pltpu.VMEM((QUAD, rows, depth), jnp.bfloat16),
                pltpu.VMEM((stages - 1, rows, depth), jnp.bfloat16),
                pltpu.VMEM((peers, 1, rows), f32),
                pltpu.VMEM((QUAD, rows, 128), f32),
                pltpu.VMEM((QUAD, rows, 128), f32),
                pltpu.VMEM((QUAD, rows, 128), f32),
                pltpu.VMEM((stages, 1, rows), f32),
                pltpu.VMEM((stages, 1, rows), f32),
                pltpu.VMEM((QUAD, 1, rows), f32),
                pltpu.VMEM((QUAD, 1, rows), f32),
                dma((stages - 1, chunks)),
                dma((chunks,)),
                dma((stages - 1, chunks)),
                dma((chunks,)), dma((chunks,)),
                dma((chunks,)), dma((chunks,)),
                dma((chunks,)), dma((chunks,)),
                dma((peers,)), dma((peers,)),
                dma((stages - 1,)), dma((stages,)),
                dma((QUAD,)), dma((QUAD,)),
            ],
            compiler_params=pltpu.CompilerParams(
                collective_id=0, has_side_effects=True, vmem_limit_bytes=48 * 1024 * 1024
            ),
        )(embeddings, cluster_ids.reshape(1, rows), live_rows)
        return weights.reshape(rows)

    return jax.shard_map(
        body,
        mesh=mesh,
        in_specs=(
            P(("groups", "blk", "inner"), None),
            P(("groups", "blk", "inner")),
            P(("groups", "blk", "inner")),
        ),
        out_specs=P(("groups", "blk", "inner")),
        check_vma=False,
    )
```

```python
import functools
import math

import jax
import jax.numpy as jnp
from jax import lax
from jax.experimental import pallas as pl
from jax.experimental.pallas import tpu as pltpu
from jax.sharding import PartitionSpec as P

sharpness = 8.0
epsilon = 1e-06
base_weight = 8.0
MESH = pl.DeviceIdType.MESH
LOG2E = 1.4426950408889634
COLS = 2
QUAD = 2 * COLS
NEG = -1e30


def kernel(
    stages, chunks, detour, emb, ids, live, out,
    quad, vis, relay_rows, tags, tag_col, cap_col, acc, vsum, rsum, gpart, gsum,
    fwd_send, own_send, vis_recv, y_send, y_recv, i_send, i_recv, d_send, d_recv,
    x_recv, o_send, h_send, t_send, t_recv, r_send, r_recv, g_send, g_recv,
):
    rows, depth = emb.shape
    span = rows // chunks
    half = stages // 2 - 1
    blk, core = lax.axis_index("blk"), lax.axis_index("inner")
    odd = lax.axis_index("groups") % 2 if detour else 0
    group = lax.axis_index("groups")

    def flip(s):
        return s + odd * (stages - 1 - 2 * s)

    stage, col = flip(blk // COLS), blk % COLS
    upper = stage // (half + 1)
    q = col * 2 + core
    me = blk * 2 + core
    peers = stages * QUAD

    def at(s, y, c):
        return {"blk": flip(s) * COLS + y, "inner": c}

    def peer_of(index):
        return {"blk": index // 2, "inner": index % 2}

    def part(k):
        return pl.ds(pl.multiple_of(k * span, span), span)

    def remote(src, dst, send, recv, device):
        return pltpu.make_async_remote_copy(
            src_ref=src, dst_ref=dst, send_sem=send, recv_sem=recv,
            device_id=device, device_id_type=MESH,
        )

    def own_forward(k):
        return remote(quad.at[q, part(k)], vis.at[0, part(k)], own_send.at[k], vis_recv.at[0, k],
                      at(stage + 1, col, core))

    def own_back(k):
        return remote(quad.at[q, part(k)], vis.at[half + 1, part(k)], own_send.at[k],
                      vis_recv.at[half + 1, k], at(stage - 1, col, core))

    def pass_forward(s, k):
        slot = s + 1 - upper
        return remote(vis.at[s, part(k)], vis.at[slot, part(k)], fwd_send.at[s, k],
                      vis_recv.at[slot, k], at(stage + 1, col, core))

    def pass_back(s, k):
        slot = half + 1 + s
        return remote(vis.at[slot, part(k)], vis.at[slot + 1, part(k)], fwd_send.at[slot, k],
                      vis_recv.at[slot + 1, k], at(stage - 1, col, core))

    def arrival(slot, k):
        return remote(vis.at[slot, part(k)], vis.at[slot, part(k)], fwd_send.at[slot, k],
                      vis_recv.at[slot, k], at(stage, col, 1 - core))

    def across(owner, k):
        return remote(quad.at[owner, part(k)], quad.at[owner, part(k)], y_send.at[k], y_recv.at[k],
                      at(stage, 1 - col, core))

    def beside(owner, k):
        return remote(quad.at[owner, part(k)], quad.at[owner, part(k)], i_send.at[k], i_recv.at[k],
                      at(stage, col, 1 - core))

    def diagonal(owner, k):
        return remote(quad.at[owner, part(k)], quad.at[owner, part(k)], d_send.at[k], d_recv.at[k],
                      at(stage, col, 1 - core))

    twin = {"groups": group + 1 - 2 * odd}

    def relay_in(k):
        return remote(vis.at[0, part(k)], relay_rows.at[part(k)], fwd_send.at[0, k], x_recv.at[k], twin)

    def relay_on(k):
        return remote(relay_rows.at[part(k)], relay_rows.at[part(k)], o_send.at[k], x_recv.at[k],
                      at(stage - 1, col, core))

    def relay_home(k):
        return remote(relay_rows.at[part(k)], vis.at[1, part(k)], h_send.at[k], vis_recv.at[1, k], twin)

    def relay_arrival(k):
        return remote(relay_rows.at[part(k)], relay_rows.at[part(k)], o_send.at[k], x_recv.at[k], twin)

    def carry(k):
        if k >= detour:
            return

        @pl.when(stage < stages - 1)
        def _():
            relay_arrival(k).wait_recv()

            @pl.when(stage < 2)
            def _():
                relay_home(k).start()

            @pl.when(stage > 0)
            def _():
                relay_on(k).start()

    def tag_copy(owner, sem, device):
        return remote(tags.at[owner], tags.at[owner], t_send.at[sem], t_recv.at[owner], device)

    q_across, q_beside = (1 - col) * 2 + core, col * 2 + 1 - core
    q_diag = (1 - col) * 2 + 1 - core

    barrier = pltpu.get_barrier_semaphore()

    def greet(p, _):
        pl.semaphore_signal(barrier, inc=1, device_id=peer_of((me + p) % peers), device_id_type=MESH)
        return 0

    lax.fori_loop(1, peers, greet, 0)
    if detour:
        pl.semaphore_signal(barrier, inc=1, device_id=twin, device_id_type=MESH)

    def normalize(k):
        wide = emb[part(k), :].astype(jnp.float32)
        scale = lax.rsqrt(jnp.mean(wide * wide, axis=1, keepdims=True) + epsilon) / math.sqrt(depth)
        quad[q, part(k), :] = (wide * scale).astype(jnp.bfloat16)

    position = lax.broadcasted_iota(jnp.int32, (1, rows), 1)
    tags[me] = jnp.where(position < live[0], ids[...], -1).astype(jnp.float32)
    normalize(0)
    pl.semaphore_wait(barrier, peers - 1 + (1 if detour else 0))

    def start_own(k):
        @pl.when(stage <= half)
        def _():
            own_forward(k).start()

        @pl.when(stage >= half + 2)
        def _():
            own_back(k).start()

        across(q, k).start()
        beside(q, k).start()

    def send_tags(p, _):
        tag_copy(me, p, peer_of((me + p) % peers)).start()
        return 0

    start_own(0)
    lax.fori_loop(1, peers, send_tags, 0)

    def rest(k, _):
        normalize(k)
        start_own(k)
        return 0

    lax.fori_loop(1, chunks, rest, 0)

    def receive(s, k):
        @pl.when(stage > s)
        def _():
            arrival(s, k).wait_recv()

            if s == 0 and k < detour:
                @pl.when(stage == 1)
                def _():
                    relay_in(k).start()

                @pl.when(stage == 2)
                def _():
                    pass_forward(s, k).start()
            elif s > 0 and k < detour:
                pass
            else:
                @pl.when(stage < stages - 1)
                def _():
                    pass_forward(s, k).start()

        if s <= stages - 3 - half:
            @pl.when((stage > half) & (stage + s < stages - 1))
            def _():
                arrival(half + 1 + s, k).wait_recv()

                @pl.when(stage >= half + 2)
                def _():
                    pass_back(s, k).start()

    for k in range(chunks):
        receive(0, k)
        across(q_across, k).wait_recv()
        diagonal(q_across, k).start()
        if k % 2 == 0 and k > 0:
            carry(k // 2 - 1)

    def take_tags(p, _):
        tag_copy((me + p) % peers, p, peer_of((me + p) % peers)).wait_recv()
        return 0

    lax.fori_loop(1, peers, take_tags, 0)
    for g in range(QUAD):
        row = tags[flip(stage) * QUAD + g]
        tall = jnp.broadcast_to(row, (128, rows)).T
        tag_col[g] = tall
        cap_col[g] = jnp.where(tall < 0, NEG, 0.0)
        acc[g] = jnp.zeros((rows, 128), jnp.float32)

    def settle(k, _):
        beside(q_beside, k).wait_recv()
        diagonal(q_diag, k).wait_recv()
        return 0

    lax.fori_loop(0, chunks, settle, 0)

    unit = rows // 2

    def visit(block, owner, slot, u, keep):
        lanes = slice(u * unit, (u + 1) * unit)
        seen = block[lanes, :]
        tag_row = tags[owner, :, lanes]
        same = jnp.where(tag_row < 0, NEG, -sharpness * LOG2E)
        other = same - 2.0
        total = jnp.zeros((8, unit), jnp.float32)
        tall = rows // 2
        for g in range(QUAD):
            for t in range(rows // tall):
                down = slice(t * tall, (t + 1) * tall)
                cosines = lax.dot_general(
                    quad[g, down, :], seen, (((1,), (1,)), ((), ())),
                    preferred_element_type=jnp.float32,
                )
                scaled = cosines * (sharpness * LOG2E)
                kept = acc[g, down, :] if keep else None
                sums = []
                for b in range(unit // 128):
                    wide = slice(b * 128, (b + 1) * 128)
                    bias = jnp.where(tag_col[g, down, :] == tag_row[:, wide], same[:, wide], other[:, wide])
                    weight = jnp.exp2(scaled[:, wide] + (bias + cap_col[g, down, :]))
                    if keep:
                        kept = kept + weight
                    sums.append(jnp.sum(weight.reshape(tall // 8, 8, 128), axis=0))
                if keep:
                    acc[g, down, :] = kept
                total = total + jnp.concatenate(sums, axis=1)
        vsum[slot, :, lanes] = jnp.sum(total, axis=0, keepdims=True)

    def owner_of(visitor):
        return flip(visitor) * QUAD + q

    def from_below(s):
        return (stage - 1) * (1 - upper) + half * upper - s

    def visit_forward(s, u):
        @pl.when(stage > s)
        def _():
            visit(vis.at[s], owner_of(from_below(s)), s, u, True)

    def visit_back(s, u):
        if s <= stages - 3 - half:
            @pl.when((stage > half) & (stage + s < stages - 1))
            def _():
                visit(vis.at[half + 1 + s], owner_of(stage + 1 + s), half + 1 + s, u, True)

    def visit_own(u):
        visit(quad.at[q], me, stages - 1, u, False)

    early = chunks // 2 + 1
    carry(3)
    visit_own(0)
    carry(4)
    visit_forward(0, 0)
    visit_back(0, 0)
    for k in range(5, detour):
        carry(k)
    for k in range(early):
        receive(1, k)
    visit_forward(1, 0)
    visit_back(1, 0)
    receive(1, early)
    visit_own(1)
    visit_forward(0, 1)
    for k in range(early + 1, chunks - 1):
        receive(1, k)
    visit_back(0, 1)
    receive(1, chunks - 1)
    visit_forward(1, 1)
    visit_back(1, 1)
    for s in range(2, half + 1):
        for u in range(2):
            for k in range(u * chunks // 2, (u + 1) * chunks // 2):
                receive(s, k)
            visit_forward(s, u)
            visit_back(s, u)

    def give_back(slot, visitor):
        return remote(vsum.at[slot], rsum.at[stage], r_send.at[slot], r_recv.at[stage],
                      at(visitor, col, core))

    def each_return(act):
        for s in range(half + 1):
            @pl.when(stage > s)
            def _():
                act(give_back(s, from_below(s)))

            if s <= stages - 3 - half:
                @pl.when((stage > half) & (stage + s < stages - 1))
                def _():
                    act(give_back(half + 1 + s, stage + 1 + s))

    each_return(lambda copy: copy.start())
    for g in range(QUAD):
        gpart[g] = jnp.sum(acc[g].T, axis=0, keepdims=True)

    def share(step):
        g = (q + step) % QUAD
        return remote(gpart.at[g], gsum.at[q], g_send.at[step], g_recv.at[q], at(stage, g // 2, g % 2))

    def shared(step):
        g = (q + step) % QUAD
        return remote(gpart.at[g], gsum.at[g], g_send.at[step], g_recv.at[g], at(stage, g // 2, g % 2))

    for step in range(1, QUAD):
        share(step).start()
    vsum[stages - 1] = vsum[stages - 1] + gpart[q]
    for other in range(stages):
        @pl.when(((stage <= half) & (other > stage)) | ((stage > other) & (other > half)))
        def _():
            remote(rsum.at[other], rsum.at[other], r_send.at[0], r_recv.at[other],
                   at(stage, col, 1 - core)).wait_recv()
            vsum[stages - 1] = vsum[stages - 1] + rsum[other]

    for step in range(1, QUAD):
        shared(step).wait_recv()
        vsum[stages - 1] = vsum[stages - 1] + gsum[(q + step) % QUAD]
    mask = (tags[me] >= 0).astype(jnp.float32)
    out[...] = mask * base_weight / (vsum[stages - 1] + 1.0 - mask)

    for k in range(chunks):
        @pl.when(stage <= half)
        def _():
            own_forward(k).wait_send()

        @pl.when(stage >= half + 2)
        def _():
            own_back(k).wait_send()

        across(q, k).wait_send()
        beside(q, k).wait_send()
        diagonal(q_across, k).wait_send()
        for s in range(half + 1):
            if s == 0 and k < detour:
                @pl.when((stage == 1) | (stage == 2))
                def _():
                    pass_forward(s, k).wait_send()
            elif s > 0 and k < detour:
                pass
            else:
                @pl.when((stage > s) & (stage < stages - 1))
                def _():
                    pass_forward(s, k).wait_send()

            if s <= stages - 3 - half:
                @pl.when((stage >= half + 2) & (stage + s < stages - 1))
                def _():
                    pass_back(s, k).wait_send()
        if k < detour:
            @pl.when(stage < 2)
            def _():
                relay_home(k).wait_send()

            @pl.when((stage > 0) & (stage < stages - 1))
            def _():
                relay_on(k).wait_send()

    def drain_tags(p, _):
        tag_copy(me, p, peer_of((me + p) % peers)).wait_send()
        return 0

    lax.fori_loop(1, peers, drain_tags, 0)
    each_return(lambda copy: copy.wait_send())
    for step in range(1, QUAD):
        share(step).wait_send()


def solution(mesh):
    stages = mesh.shape["blk"] // COLS

    def body(embeddings, cluster_ids, live_rows):
        rows, depth = embeddings.shape
        chunks = 8
        detour = 5 if stages == 4 and mesh.shape["groups"] % 2 == 0 else 0
        peers = stages * QUAD
        dma = pltpu.SemaphoreType.DMA
        f32 = jnp.float32
        weights = pl.pallas_call(
            functools.partial(kernel, stages, chunks, detour),
            out_shape=jax.ShapeDtypeStruct((1, rows), f32),
            in_specs=[
                pl.BlockSpec(memory_space=pltpu.VMEM),
                pl.BlockSpec(memory_space=pltpu.VMEM),
                pl.BlockSpec(memory_space=pltpu.SMEM),
            ],
            out_specs=pl.BlockSpec(memory_space=pltpu.VMEM),
            scratch_shapes=[
                pltpu.VMEM((QUAD, rows, depth), jnp.bfloat16),
                pltpu.VMEM((stages - 1, rows, depth), jnp.bfloat16),
                pltpu.VMEM((rows, depth), jnp.bfloat16),
                pltpu.VMEM((peers, 1, rows), f32),
                pltpu.VMEM((QUAD, rows, 128), f32),
                pltpu.VMEM((QUAD, rows, 128), f32),
                pltpu.VMEM((QUAD, rows, 128), f32),
                pltpu.VMEM((stages, 1, rows), f32),
                pltpu.VMEM((stages, 1, rows), f32),
                pltpu.VMEM((QUAD, 1, rows), f32),
                pltpu.VMEM((QUAD, 1, rows), f32),
                dma((stages - 1, chunks)),
                dma((chunks,)),
                dma((stages - 1, chunks)),
                dma((chunks,)), dma((chunks,)),
                dma((chunks,)), dma((chunks,)),
                dma((chunks,)), dma((chunks,)),
                dma((chunks,)), dma((chunks,)), dma((chunks,)),
                dma((peers,)), dma((peers,)),
                dma((stages - 1,)), dma((stages,)),
                dma((QUAD,)), dma((QUAD,)),
            ],
            compiler_params=pltpu.CompilerParams(
                collective_id=0, has_side_effects=True, vmem_limit_bytes=48 * 1024 * 1024
            ),
        )(embeddings, cluster_ids.reshape(1, rows), live_rows)
        return weights.reshape(rows)

    return jax.shard_map(
        body,
        mesh=mesh,
        in_specs=(
            P(("groups", "blk", "inner"), None),
            P(("groups", "blk", "inner")),
            P(("groups", "blk", "inner")),
        ),
        out_specs=P(("groups", "blk", "inner")),
        check_vma=False,
    )
```

```python
import functools
import math

import jax
import jax.numpy as jnp
from jax import lax
from jax.experimental import pallas as pl
from jax.experimental.pallas import tpu as pltpu
from jax.sharding import PartitionSpec as P

sharpness = 8.0
epsilon = 1e-06
base_weight = 8.0
MESH = pl.DeviceIdType.MESH
LOG2E = 1.4426950408889634
COLS = 2
QUAD = 2 * COLS
NEG = -1e30


def kernel(
    stages, chunks, detour, emb, ids, live, out,
    staged, e_sem, quad, vis, relay_rows, tags, tag_col, cap_col, acc, vsum, rsum, gpart, gsum,
    fwd_send, own_send, vis_recv, y_send, y_recv, i_send, i_recv, d_send, d_recv,
    x_recv, o_send, h_send, t_send, t_recv, r_send, r_recv, g_send, g_recv,
):
    rows, depth = emb.shape
    span = rows // chunks
    half = stages // 2 - 1
    blk, core = lax.axis_index("blk"), lax.axis_index("inner")
    odd = lax.axis_index("groups") % 2 if detour else 0
    group = lax.axis_index("groups")

    def flip(s):
        return s + odd * (stages - 1 - 2 * s)

    stage, col = flip(blk // COLS), blk % COLS
    upper = stage // (half + 1)
    q = col * 2 + core
    me = blk * 2 + core
    peers = stages * QUAD

    def at(s, y, c):
        return {"blk": flip(s) * COLS + y, "inner": c}

    def peer_of(index):
        return {"blk": index // 2, "inner": index % 2}

    def part(k):
        return pl.ds(pl.multiple_of(k * span, span), span)

    def remote(src, dst, send, recv, device):
        return pltpu.make_async_remote_copy(
            src_ref=src, dst_ref=dst, send_sem=send, recv_sem=recv,
            device_id=device, device_id_type=MESH,
        )

    def own_forward(k):
        return remote(quad.at[q, part(k)], vis.at[0, part(k)], own_send.at[k], vis_recv.at[0, k],
                      at(stage + 1, col, core))

    def own_back(k):
        return remote(quad.at[q, part(k)], vis.at[half + 1, part(k)], own_send.at[k],
                      vis_recv.at[half + 1, k], at(stage - 1, col, core))

    def pass_forward(s, k):
        slot = s + 1 - upper
        return remote(vis.at[s, part(k)], vis.at[slot, part(k)], fwd_send.at[s, k],
                      vis_recv.at[slot, k], at(stage + 1, col, core))

    def pass_back(s, k):
        slot = half + 1 + s
        return remote(vis.at[slot, part(k)], vis.at[slot + 1, part(k)], fwd_send.at[slot, k],
                      vis_recv.at[slot + 1, k], at(stage - 1, col, core))

    def arrival(slot, k):
        return remote(vis.at[slot, part(k)], vis.at[slot, part(k)], fwd_send.at[slot, k],
                      vis_recv.at[slot, k], at(stage, col, 1 - core))

    def across(owner, k):
        return remote(quad.at[owner, part(k)], quad.at[owner, part(k)], y_send.at[k], y_recv.at[k],
                      at(stage, 1 - col, core))

    def beside(owner, k):
        return remote(quad.at[owner, part(k)], quad.at[owner, part(k)], i_send.at[k], i_recv.at[k],
                      at(stage, col, 1 - core))

    def diagonal(owner, k):
        return remote(quad.at[owner, part(k)], quad.at[owner, part(k)], d_send.at[k], d_recv.at[k],
                      at(stage, col, 1 - core))

    twin = {"groups": group + 1 - 2 * odd}

    def relay_in(k):
        return remote(vis.at[0, part(k)], relay_rows.at[part(k)], fwd_send.at[0, k], x_recv.at[k], twin)

    def relay_on(k):
        return remote(relay_rows.at[part(k)], relay_rows.at[part(k)], o_send.at[k], x_recv.at[k],
                      at(stage - 1, col, core))

    def relay_home(k):
        return remote(relay_rows.at[part(k)], vis.at[1, part(k)], h_send.at[k], vis_recv.at[1, k], twin)

    def relay_arrival(k):
        return remote(relay_rows.at[part(k)], relay_rows.at[part(k)], o_send.at[k], x_recv.at[k], twin)

    def carry(k, role):
        if k < 0 or k >= detour:
            return

        @pl.when(stage == role)
        def _():
            relay_arrival(k).wait_recv()

            @pl.when(stage < 2)
            def _():
                relay_home(k).start()

            @pl.when(stage > 0)
            def _():
                relay_on(k).start()

    def tag_copy(owner, sem, device):
        return remote(tags.at[owner], tags.at[owner], t_send.at[sem], t_recv.at[owner], device)

    q_across, q_beside = (1 - col) * 2 + core, col * 2 + 1 - core
    q_diag = (1 - col) * 2 + 1 - core

    def load(k):
        return pltpu.make_async_copy(emb.at[part(k)], staged.at[part(k)], e_sem.at[k])

    for k in range(chunks):
        load(k).start()
    barrier = pltpu.get_barrier_semaphore()

    def greet(p, _):
        pl.semaphore_signal(barrier, inc=1, device_id=peer_of((me + p) % peers), device_id_type=MESH)
        return 0

    lax.fori_loop(1, peers, greet, 0)
    if detour:
        pl.semaphore_signal(barrier, inc=1, device_id=twin, device_id_type=MESH)

    def normalize(k):
        load(k).wait()
        wide = staged[part(k), :].astype(jnp.float32)
        scale = lax.rsqrt(jnp.mean(wide * wide, axis=1, keepdims=True) + epsilon) / math.sqrt(depth)
        quad[q, part(k), :] = (wide * scale).astype(jnp.bfloat16)

    position = lax.broadcasted_iota(jnp.int32, (1, rows), 1)
    tags[me] = jnp.where(position < live[0], ids[...], -1).astype(jnp.float32)
    normalize(0)
    pl.semaphore_wait(barrier, peers - 1 + (1 if detour else 0))

    def start_own(k):
        @pl.when(stage <= half)
        def _():
            own_forward(k).start()

        @pl.when(stage >= half + 2)
        def _():
            own_back(k).start()

        across(q, k).start()
        beside(q, k).start()

    def send_tags(p, _):
        tag_copy(me, p, peer_of((me + p) % peers)).start()
        return 0

    start_own(0)
    lax.fori_loop(1, peers, send_tags, 0)

    def rest(k, _):
        normalize(k)
        start_own(k)
        return 0

    lax.fori_loop(1, chunks, rest, 0)

    def receive(s, k):
        @pl.when(stage > s)
        def _():
            arrival(s, k).wait_recv()

            if s == 0 and k < detour:
                @pl.when(stage == 1)
                def _():
                    relay_in(k).start()

                @pl.when(stage == 2)
                def _():
                    pass_forward(s, k).start()
            elif s > 0 and k < detour:
                pass
            else:
                @pl.when(stage < stages - 1)
                def _():
                    pass_forward(s, k).start()

        if s <= stages - 3 - half:
            @pl.when((stage > half) & (stage + s < stages - 1))
            def _():
                arrival(half + 1 + s, k).wait_recv()

                @pl.when(stage >= half + 2)
                def _():
                    pass_back(s, k).start()

    def take_tags(p, _):
        tag_copy((me + p) % peers, p, peer_of((me + p) % peers)).wait_recv()
        return 0

    def lay_tags(g):
        row = tags[flip(stage) * QUAD + g]
        tall = jnp.broadcast_to(row, (128, rows)).T
        tag_col[g] = tall
        cap_col[g] = jnp.where(tall < 0, NEG, 0.0)
        acc[g] = jnp.zeros((rows, 128), jnp.float32)

    for k in range(chunks):
        if k == 2:
            lax.fori_loop(1, peers, take_tags, 0)
        if 2 <= k < 2 + QUAD:
            lay_tags(k - 2)
        receive(0, k)
        across(q_across, k).wait_recv()
        diagonal(q_across, k).start()
        carry(k - 1, 2)
        carry(k - 2, 1)
        carry(k - 3, 0)

    def settle(k, _):
        beside(q_beside, k).wait_recv()
        diagonal(q_diag, k).wait_recv()
        return 0

    lax.fori_loop(0, chunks, settle, 0)

    third = rows // 2 + rows // 4
    bounds = {0: (0, rows // 2), 1: (rows // 2, rows), 2: (rows // 2, third), 3: (third, rows)}

    def visit(block, owner, slot, u, keep):
        low, high = bounds[u]
        unit = high - low
        lanes = slice(low, high)
        seen = block[lanes, :]
        tag_row = tags[owner, :, lanes]
        same = jnp.where(tag_row < 0, NEG, -sharpness * LOG2E)
        other = same - 2.0
        total = jnp.zeros((8, unit), jnp.float32)
        tall = rows // 2
        for g in range(QUAD):
            for t in range(rows // tall):
                down = slice(t * tall, (t + 1) * tall)
                cosines = lax.dot_general(
                    quad[g, down, :], seen, (((1,), (1,)), ((), ())),
                    preferred_element_type=jnp.float32,
                )
                scaled = cosines * (sharpness * LOG2E)
                kept = acc[g, down, :] if keep else None
                sums = []
                for b in range(unit // 128):
                    wide = slice(b * 128, (b + 1) * 128)
                    bias = jnp.where(tag_col[g, down, :] == tag_row[:, wide], same[:, wide], other[:, wide])
                    weight = jnp.exp2(scaled[:, wide] + (bias + cap_col[g, down, :]))
                    if keep:
                        kept = kept + weight
                    sums.append(jnp.sum(weight.reshape(tall // 8, 8, 128), axis=0))
                if keep:
                    acc[g, down, :] = kept
                total = total + jnp.concatenate(sums, axis=1)
        vsum[slot, :, lanes] = jnp.sum(total, axis=0, keepdims=True)

    def owner_of(visitor):
        return flip(visitor) * QUAD + q

    def from_below(s):
        return (stage - 1) * (1 - upper) + half * upper - s

    def visit_forward(s, u):
        @pl.when(stage > s)
        def _():
            visit(vis.at[s], owner_of(from_below(s)), s, u, True)

    def visit_back(s, u):
        if s <= stages - 3 - half:
            @pl.when((stage > half) & (stage + s < stages - 1))
            def _():
                visit(vis.at[half + 1 + s], owner_of(stage + 1 + s), half + 1 + s, u, True)

    def visit_own(u):
        visit(quad.at[q], me, stages - 1, u, False)

    for k in range(chunks, chunks + 3):
        carry(k - 1, 2)
        carry(k - 2, 1)
        carry(k - 3, 0)
    visit_own(0)
    direct = list(range(detour, chunks)) if detour else []
    waiting = [k for k in range(chunks) if k not in direct]
    for k in direct[:1]:
        receive(1, k)
    visit_forward(0, 0)
    visit_back(0, 0)
    for k in direct[1:2]:
        receive(1, k)
    for k in waiting[:chunks // 2]:
        receive(1, k)
    visit_forward(1, 0)
    visit_back(1, 0)
    visit_own(1)
    visit_forward(0, 1)
    for k in direct[2:]:
        receive(1, k)
    visit_back(0, 1)
    for k in waiting[chunks // 2:]:
        if k < third // span:
            receive(1, k)
    visit_forward(1, 2)
    visit_back(1, 2)
    for k in waiting[chunks // 2:]:
        if k >= third // span:
            receive(1, k)
    visit_forward(1, 3)
    visit_back(1, 3)
    for s in range(2, half + 1):
        for u in range(2):
            for k in range(u * chunks // 2, (u + 1) * chunks // 2):
                receive(s, k)
            visit_forward(s, u)
            visit_back(s, u)

    def give_back(slot, visitor):
        return remote(vsum.at[slot], rsum.at[stage], r_send.at[slot], r_recv.at[stage],
                      at(visitor, col, core))

    def each_return(act):
        for s in range(half + 1):
            @pl.when(stage > s)
            def _():
                act(give_back(s, from_below(s)))

            if s <= stages - 3 - half:
                @pl.when((stage > half) & (stage + s < stages - 1))
                def _():
                    act(give_back(half + 1 + s, stage + 1 + s))

    each_return(lambda copy: copy.start())
    for g in range(QUAD):
        gpart[g] = jnp.sum(acc[g].T, axis=0, keepdims=True)

    def share(step):
        g = (q + step) % QUAD
        return remote(gpart.at[g], gsum.at[q], g_send.at[step], g_recv.at[q], at(stage, g // 2, g % 2))

    def shared(step):
        g = (q + step) % QUAD
        return remote(gpart.at[g], gsum.at[g], g_send.at[step], g_recv.at[g], at(stage, g // 2, g % 2))

    for step in range(1, QUAD):
        share(step).start()
    vsum[stages - 1] = vsum[stages - 1] + gpart[q]
    for other in range(stages):
        @pl.when(((stage <= half) & (other > stage)) | ((stage > other) & (other > half)))
        def _():
            remote(rsum.at[other], rsum.at[other], r_send.at[0], r_recv.at[other],
                   at(stage, col, 1 - core)).wait_recv()
            vsum[stages - 1] = vsum[stages - 1] + rsum[other]

    for step in range(1, QUAD):
        shared(step).wait_recv()
        vsum[stages - 1] = vsum[stages - 1] + gsum[(q + step) % QUAD]
    mask = (tags[me] >= 0).astype(jnp.float32)
    out[...] = mask * base_weight / (vsum[stages - 1] + 1.0 - mask)

    for k in range(chunks):
        @pl.when(stage <= half)
        def _():
            own_forward(k).wait_send()

        @pl.when(stage >= half + 2)
        def _():
            own_back(k).wait_send()

        across(q, k).wait_send()
        beside(q, k).wait_send()
        diagonal(q_across, k).wait_send()
        for s in range(half + 1):
            if s == 0 and k < detour:
                @pl.when((stage == 1) | (stage == 2))
                def _():
                    pass_forward(s, k).wait_send()
            elif s > 0 and k < detour:
                pass
            else:
                @pl.when((stage > s) & (stage < stages - 1))
                def _():
                    pass_forward(s, k).wait_send()

            if s <= stages - 3 - half:
                @pl.when((stage >= half + 2) & (stage + s < stages - 1))
                def _():
                    pass_back(s, k).wait_send()
        if k < detour:
            @pl.when(stage < 2)
            def _():
                relay_home(k).wait_send()

            @pl.when((stage > 0) & (stage < stages - 1))
            def _():
                relay_on(k).wait_send()

    def drain_tags(p, _):
        tag_copy(me, p, peer_of((me + p) % peers)).wait_send()
        return 0

    lax.fori_loop(1, peers, drain_tags, 0)
    each_return(lambda copy: copy.wait_send())
    for step in range(1, QUAD):
        share(step).wait_send()


def solution(mesh):
    stages = mesh.shape["blk"] // COLS

    def body(embeddings, cluster_ids, live_rows):
        rows, depth = embeddings.shape
        chunks = 8
        detour = 5 if stages == 4 and mesh.shape["groups"] % 2 == 0 else 0
        peers = stages * QUAD
        dma = pltpu.SemaphoreType.DMA
        f32 = jnp.float32
        weights = pl.pallas_call(
            functools.partial(kernel, stages, chunks, detour),
            out_shape=jax.ShapeDtypeStruct((1, rows), f32),
            in_specs=[
                pl.BlockSpec(memory_space=pl.ANY),
                pl.BlockSpec(memory_space=pltpu.VMEM),
                pl.BlockSpec(memory_space=pltpu.SMEM),
            ],
            out_specs=pl.BlockSpec(memory_space=pltpu.VMEM),
            scratch_shapes=[
                pltpu.VMEM((rows, depth), jnp.bfloat16),
                dma((chunks,)),
                pltpu.VMEM((QUAD, rows, depth), jnp.bfloat16),
                pltpu.VMEM((stages - 1, rows, depth), jnp.bfloat16),
                pltpu.VMEM((rows, depth), jnp.bfloat16),
                pltpu.VMEM((peers, 1, rows), f32),
                pltpu.VMEM((QUAD, rows, 128), f32),
                pltpu.VMEM((QUAD, rows, 128), f32),
                pltpu.VMEM((QUAD, rows, 128), f32),
                pltpu.VMEM((stages, 1, rows), f32),
                pltpu.VMEM((stages, 1, rows), f32),
                pltpu.VMEM((QUAD, 1, rows), f32),
                pltpu.VMEM((QUAD, 1, rows), f32),
                dma((stages - 1, chunks)),
                dma((chunks,)),
                dma((stages - 1, chunks)),
                dma((chunks,)), dma((chunks,)),
                dma((chunks,)), dma((chunks,)),
                dma((chunks,)), dma((chunks,)),
                dma((chunks,)), dma((chunks,)), dma((chunks,)),
                dma((peers,)), dma((peers,)),
                dma((stages - 1,)), dma((stages,)),
                dma((QUAD,)), dma((QUAD,)),
            ],
            compiler_params=pltpu.CompilerParams(
                collective_id=0, has_side_effects=True, vmem_limit_bytes=48 * 1024 * 1024
            ),
        )(embeddings, cluster_ids.reshape(1, rows), live_rows)
        return weights.reshape(rows)

    return jax.shard_map(
        body,
        mesh=mesh,
        in_specs=(
            P(("groups", "blk", "inner"), None),
            P(("groups", "blk", "inner")),
            P(("groups", "blk", "inner")),
        ),
        out_specs=P(("groups", "blk", "inner")),
        check_vma=False,
    )
```

```python
import functools
import math

import jax
import jax.numpy as jnp
from jax import lax
from jax.experimental import pallas as pl
from jax.experimental.pallas import tpu as pltpu
from jax.sharding import PartitionSpec as P

sharpness = 8.0
epsilon = 1e-06
base_weight = 8.0
MESH = pl.DeviceIdType.MESH
LOG2E = 1.4426950408889634
COLS = 2
QUAD = 2 * COLS
NEG = -1e30


def kernel(
    stages, chunks, detour, emb, ids, live, out,
    staged, e_sem, quad, vis, relay_rows, tags, tag_col, cap_col, acc, vsum, rsum, gpart, gsum,
    fwd_send, own_send, vis_recv, y_send, y_recv, i_send, i_recv, d_send, d_recv,
    n_send, x_recv, o_send, h_send, t_send, t_recv, r_send, r_recv, g_send, g_recv,
):
    rows, depth = emb.shape
    span = rows // chunks
    half = stages // 2 - 1
    blk, core = lax.axis_index("blk"), lax.axis_index("inner")
    odd = lax.axis_index("groups") % 2 if detour else 0
    group = lax.axis_index("groups")

    def flip(s):
        return s + odd * (stages - 1 - 2 * s)

    stage, col = flip(blk // COLS), blk % COLS
    upper = stage // (half + 1)
    q = col * 2 + core
    me = blk * 2 + core
    peers = stages * QUAD

    def at(s, y, c):
        return {"blk": flip(s) * COLS + y, "inner": c}

    def peer_of(index):
        return {"blk": index // 2, "inner": index % 2}

    def part(k):
        return pl.ds(pl.multiple_of(k * span, span), span)

    def remote(src, dst, send, recv, device):
        return pltpu.make_async_remote_copy(
            src_ref=src, dst_ref=dst, send_sem=send, recv_sem=recv,
            device_id=device, device_id_type=MESH,
        )

    def own_forward(k):
        return remote(quad.at[q, part(k)], vis.at[0, part(k)], own_send.at[k], vis_recv.at[0, k],
                      at(stage + 1, col, core))

    def own_back(k):
        return remote(quad.at[q, part(k)], vis.at[half + 1, part(k)], own_send.at[k],
                      vis_recv.at[half + 1, k], at(stage - 1, col, core))

    def pass_forward(s, k):
        slot = s + 1 - upper
        return remote(vis.at[s, part(k)], vis.at[slot, part(k)], fwd_send.at[s, k],
                      vis_recv.at[slot, k], at(stage + 1, col, core))

    def pass_back(s, k):
        slot = half + 1 + s
        return remote(vis.at[slot, part(k)], vis.at[slot + 1, part(k)], fwd_send.at[slot, k],
                      vis_recv.at[slot + 1, k], at(stage - 1, col, core))

    def arrival(slot, k):
        return remote(vis.at[slot, part(k)], vis.at[slot, part(k)], fwd_send.at[slot, k],
                      vis_recv.at[slot, k], at(stage, col, 1 - core))

    def across(owner, k):
        return remote(quad.at[owner, part(k)], quad.at[owner, part(k)], y_send.at[k], y_recv.at[k],
                      at(stage, 1 - col, core))

    def beside(owner, k):
        return remote(quad.at[owner, part(k)], quad.at[owner, part(k)], i_send.at[k], i_recv.at[k],
                      at(stage, col, 1 - core))

    def diagonal(owner, k):
        return remote(quad.at[owner, part(k)], quad.at[owner, part(k)], d_send.at[k], d_recv.at[k],
                      at(stage, col, 1 - core))

    entering = 2 if detour else 0
    twin = {"groups": group + 1 - 2 * odd}

    def relay_in(k):
        return remote(vis.at[0, part(k)], relay_rows.at[part(k)], fwd_send.at[0, k], x_recv.at[k], twin)

    def relay_enter(k):
        return remote(quad.at[q, part(k)], relay_rows.at[part(k)], n_send.at[k], x_recv.at[k], twin)

    def relay_on(k):
        return remote(relay_rows.at[part(k)], relay_rows.at[part(k)], o_send.at[k], x_recv.at[k],
                      at(stage - 1, col, core))

    def relay_home(k):
        return remote(relay_rows.at[part(k)], vis.at[1, part(k)], h_send.at[k], vis_recv.at[1, k], twin)

    def relay_arrival(k):
        return remote(relay_rows.at[part(k)], relay_rows.at[part(k)], o_send.at[k], x_recv.at[k], twin)

    def carry(k, role):
        if k < 0 or k >= detour:
            return

        @pl.when(stage == role)
        def _():
            relay_arrival(k).wait_recv()

            @pl.when(stage < 2)
            def _():
                relay_home(k).start()

            @pl.when(stage > 0)
            def _():
                relay_on(k).start()

    def tag_copy(owner, sem, device):
        return remote(tags.at[owner], tags.at[owner], t_send.at[sem], t_recv.at[owner], device)

    q_across, q_beside = (1 - col) * 2 + core, col * 2 + 1 - core
    q_diag = (1 - col) * 2 + 1 - core

    def load(k):
        return pltpu.make_async_copy(emb.at[part(k)], staged.at[part(k)], e_sem.at[k])

    for k in range(chunks):
        load(k).start()
    barrier = pltpu.get_barrier_semaphore()

    def greet(p, _):
        pl.semaphore_signal(barrier, inc=1, device_id=peer_of((me + p) % peers), device_id_type=MESH)
        return 0

    lax.fori_loop(1, peers, greet, 0)
    if detour:
        pl.semaphore_signal(barrier, inc=1, device_id=twin, device_id_type=MESH)

    def normalize(k):
        load(k).wait()
        wide = staged[part(k), :].astype(jnp.float32)
        scale = lax.rsqrt(jnp.mean(wide * wide, axis=1, keepdims=True) + epsilon) / math.sqrt(depth)
        quad[q, part(k), :] = (wide * scale).astype(jnp.bfloat16)

    position = lax.broadcasted_iota(jnp.int32, (1, rows), 1)
    tags[me] = jnp.where(position < live[0], ids[...], -1).astype(jnp.float32)
    normalize(0)
    pl.semaphore_wait(barrier, peers - 1 + (1 if detour else 0))

    def start_own(k):
        @pl.when(stage <= half)
        def _():
            own_forward(k).start()

        @pl.when(stage >= half + 2)
        def _():
            own_back(k).start()

        if detour:
            @pl.when((stage == 0) & (k < entering))
            def _():
                relay_enter(k).start()

        across(q, k).start()
        beside(q, k).start()

    def send_tags(p, _):
        tag_copy(me, p, peer_of((me + p) % peers)).start()
        return 0

    start_own(0)
    lax.fori_loop(1, peers, send_tags, 0)

    def rest(k, _):
        normalize(k)
        start_own(k)
        return 0

    lax.fori_loop(1, chunks, rest, 0)

    def receive(s, k):
        @pl.when(stage > s)
        def _():
            arrival(s, k).wait_recv()

            if s == 0 and k < detour:
                if k >= entering:
                    @pl.when(stage == 1)
                    def _():
                        relay_in(k).start()

                @pl.when(stage == 2)
                def _():
                    pass_forward(s, k).start()
            elif s > 0 and k < detour:
                pass
            else:
                @pl.when(stage < stages - 1)
                def _():
                    pass_forward(s, k).start()

        if s <= stages - 3 - half:
            @pl.when((stage > half) & (stage + s < stages - 1))
            def _():
                arrival(half + 1 + s, k).wait_recv()

                @pl.when(stage >= half + 2)
                def _():
                    pass_back(s, k).start()

    def take_tags(p, _):
        tag_copy((me + p) % peers, p, peer_of((me + p) % peers)).wait_recv()
        return 0

    def lay_tags(g):
        row = tags[flip(stage) * QUAD + g]
        tall = jnp.broadcast_to(row, (128, rows)).T
        tag_col[g] = tall
        cap_col[g] = jnp.where(tall < 0, NEG, 0.0)
        acc[g] = jnp.zeros((rows, 128), jnp.float32)

    for k in range(chunks):
        if k == 2:
            lax.fori_loop(1, peers, take_tags, 0)
        if 2 <= k < 2 + QUAD:
            lay_tags(k - 2)
        if k < entering:
            carry(k, 3)
        receive(0, k)
        across(q_across, k).wait_recv()
        diagonal(q_across, k).start()
        carry(k - 1, 2)
        carry(k - 2, 1)
        carry(k - 3, 0)

    def settle(k, _):
        beside(q_beside, k).wait_recv()
        diagonal(q_diag, k).wait_recv()
        return 0

    lax.fori_loop(0, chunks, settle, 0)

    third = rows // 2 + rows // 4
    bounds = {0: (0, rows // 2), 1: (rows // 2, rows), 2: (rows // 2, third), 3: (third, rows)}

    def visit(block, owner, slot, u, keep):
        low, high = bounds[u]
        unit = high - low
        lanes = slice(low, high)
        seen = block[lanes, :]
        tag_row = tags[owner, :, lanes]
        same = jnp.where(tag_row < 0, NEG, -sharpness * LOG2E)
        other = same - 2.0
        total = jnp.zeros((8, unit), jnp.float32)
        tall = rows // 2
        for g in range(QUAD):
            for t in range(rows // tall):
                down = slice(t * tall, (t + 1) * tall)
                cosines = lax.dot_general(
                    quad[g, down, :], seen, (((1,), (1,)), ((), ())),
                    preferred_element_type=jnp.float32,
                )
                scaled = cosines * (sharpness * LOG2E)
                kept = acc[g, down, :] if keep else None
                sums = []
                for b in range(unit // 128):
                    wide = slice(b * 128, (b + 1) * 128)
                    bias = jnp.where(tag_col[g, down, :] == tag_row[:, wide], same[:, wide], other[:, wide])
                    weight = jnp.exp2(scaled[:, wide] + (bias + cap_col[g, down, :]))
                    if keep:
                        kept = kept + weight
                    sums.append(jnp.sum(weight.reshape(tall // 8, 8, 128), axis=0))
                if keep:
                    acc[g, down, :] = kept
                total = total + jnp.concatenate(sums, axis=1)
        vsum[slot, :, lanes] = jnp.sum(total, axis=0, keepdims=True)

    def owner_of(visitor):
        return flip(visitor) * QUAD + q

    def from_below(s):
        return (stage - 1) * (1 - upper) + half * upper - s

    def visit_forward(s, u):
        @pl.when(stage > s)
        def _():
            visit(vis.at[s], owner_of(from_below(s)), s, u, True)

    def visit_back(s, u):
        if s <= stages - 3 - half:
            @pl.when((stage > half) & (stage + s < stages - 1))
            def _():
                visit(vis.at[half + 1 + s], owner_of(stage + 1 + s), half + 1 + s, u, True)

    def visit_own(u):
        visit(quad.at[q], me, stages - 1, u, False)

    for k in range(chunks, chunks + 3):
        carry(k - 1, 2)
        carry(k - 2, 1)
        carry(k - 3, 0)
    visit_own(0)
    direct = list(range(detour, chunks)) if detour else []
    waiting = [k for k in range(chunks) if k not in direct]
    for k in direct[:1]:
        receive(1, k)
    visit_forward(0, 0)
    visit_back(0, 0)
    for k in direct[1:2]:
        receive(1, k)
    for k in waiting[:chunks // 2]:
        receive(1, k)
    visit_forward(1, 0)
    visit_back(1, 0)
    visit_own(1)
    visit_forward(0, 1)
    for k in direct[2:]:
        receive(1, k)
    visit_back(0, 1)
    for k in waiting[chunks // 2:]:
        if k < third // span:
            receive(1, k)
    visit_forward(1, 2)
    visit_back(1, 2)
    for k in waiting[chunks // 2:]:
        if k >= third // span:
            receive(1, k)
    visit_forward(1, 3)
    visit_back(1, 3)
    for s in range(2, half + 1):
        for u in range(2):
            for k in range(u * chunks // 2, (u + 1) * chunks // 2):
                receive(s, k)
            visit_forward(s, u)
            visit_back(s, u)

    def give_back(slot, visitor):
        return remote(vsum.at[slot], rsum.at[stage], r_send.at[slot], r_recv.at[stage],
                      at(visitor, col, core))

    def each_return(act):
        for s in range(half + 1):
            @pl.when(stage > s)
            def _():
                act(give_back(s, from_below(s)))

            if s <= stages - 3 - half:
                @pl.when((stage > half) & (stage + s < stages - 1))
                def _():
                    act(give_back(half + 1 + s, stage + 1 + s))

    each_return(lambda copy: copy.start())
    for g in range(QUAD):
        gpart[g] = jnp.sum(acc[g].T, axis=0, keepdims=True)

    def share(step):
        g = (q + step) % QUAD
        return remote(gpart.at[g], gsum.at[q], g_send.at[step], g_recv.at[q], at(stage, g // 2, g % 2))

    def shared(step):
        g = (q + step) % QUAD
        return remote(gpart.at[g], gsum.at[g], g_send.at[step], g_recv.at[g], at(stage, g // 2, g % 2))

    for step in range(1, QUAD):
        share(step).start()
    vsum[stages - 1] = vsum[stages - 1] + gpart[q]
    for other in range(stages):
        @pl.when(((stage <= half) & (other > stage)) | ((stage > other) & (other > half)))
        def _():
            remote(rsum.at[other], rsum.at[other], r_send.at[0], r_recv.at[other],
                   at(stage, col, 1 - core)).wait_recv()
            vsum[stages - 1] = vsum[stages - 1] + rsum[other]

    for step in range(1, QUAD):
        shared(step).wait_recv()
        vsum[stages - 1] = vsum[stages - 1] + gsum[(q + step) % QUAD]
    mask = (tags[me] >= 0).astype(jnp.float32)
    out[...] = mask * base_weight / (vsum[stages - 1] + 1.0 - mask)

    for k in range(chunks):
        @pl.when(stage <= half)
        def _():
            own_forward(k).wait_send()

        @pl.when(stage >= half + 2)
        def _():
            own_back(k).wait_send()

        across(q, k).wait_send()
        beside(q, k).wait_send()
        diagonal(q_across, k).wait_send()
        for s in range(half + 1):
            if s == 0 and k < detour:
                @pl.when(((stage == 1) & (k >= entering)) | (stage == 2))
                def _():
                    pass_forward(s, k).wait_send()
            elif s > 0 and k < detour:
                pass
            else:
                @pl.when((stage > s) & (stage < stages - 1))
                def _():
                    pass_forward(s, k).wait_send()

            if s <= stages - 3 - half:
                @pl.when((stage >= half + 2) & (stage + s < stages - 1))
                def _():
                    pass_back(s, k).wait_send()
        if k < detour:
            @pl.when(stage < 2)
            def _():
                relay_home(k).wait_send()

            @pl.when((stage > 0) & ((stage < stages - 1) | (k < entering)))
            def _():
                relay_on(k).wait_send()

            @pl.when((stage == 0) & (k < entering))
            def _():
                relay_enter(k).wait_send()

    def drain_tags(p, _):
        tag_copy(me, p, peer_of((me + p) % peers)).wait_send()
        return 0

    lax.fori_loop(1, peers, drain_tags, 0)
    each_return(lambda copy: copy.wait_send())
    for step in range(1, QUAD):
        share(step).wait_send()


def solution(mesh):
    stages = mesh.shape["blk"] // COLS

    def body(embeddings, cluster_ids, live_rows):
        rows, depth = embeddings.shape
        chunks = 8
        detour = 6 if stages == 4 and mesh.shape["groups"] % 2 == 0 else 0
        peers = stages * QUAD
        dma = pltpu.SemaphoreType.DMA
        f32 = jnp.float32
        weights = pl.pallas_call(
            functools.partial(kernel, stages, chunks, detour),
            out_shape=jax.ShapeDtypeStruct((1, rows), f32),
            in_specs=[
                pl.BlockSpec(memory_space=pl.ANY),
                pl.BlockSpec(memory_space=pltpu.VMEM),
                pl.BlockSpec(memory_space=pltpu.SMEM),
            ],
            out_specs=pl.BlockSpec(memory_space=pltpu.VMEM),
            scratch_shapes=[
                pltpu.VMEM((rows, depth), jnp.bfloat16),
                dma((chunks,)),
                pltpu.VMEM((QUAD, rows, depth), jnp.bfloat16),
                pltpu.VMEM((stages - 1, rows, depth), jnp.bfloat16),
                pltpu.VMEM((rows, depth), jnp.bfloat16),
                pltpu.VMEM((peers, 1, rows), f32),
                pltpu.VMEM((QUAD, rows, 128), f32),
                pltpu.VMEM((QUAD, rows, 128), f32),
                pltpu.VMEM((QUAD, rows, 128), f32),
                pltpu.VMEM((stages, 1, rows), f32),
                pltpu.VMEM((stages, 1, rows), f32),
                pltpu.VMEM((QUAD, 1, rows), f32),
                pltpu.VMEM((QUAD, 1, rows), f32),
                dma((stages - 1, chunks)),
                dma((chunks,)),
                dma((stages - 1, chunks)),
                dma((chunks,)), dma((chunks,)),
                dma((chunks,)), dma((chunks,)),
                dma((chunks,)), dma((chunks,)),
                dma((chunks,)), dma((chunks,)), dma((chunks,)), dma((chunks,)),
                dma((peers,)), dma((peers,)),
                dma((stages - 1,)), dma((stages,)),
                dma((QUAD,)), dma((QUAD,)),
            ],
            compiler_params=pltpu.CompilerParams(
                collective_id=0, has_side_effects=True, vmem_limit_bytes=48 * 1024 * 1024
            ),
        )(embeddings, cluster_ids.reshape(1, rows), live_rows)
        return weights.reshape(rows)

    return jax.shard_map(
        body,
        mesh=mesh,
        in_specs=(
            P(("groups", "blk", "inner"), None),
            P(("groups", "blk", "inner")),
            P(("groups", "blk", "inner")),
        ),
        out_specs=P(("groups", "blk", "inner")),
        check_vma=False,
    )
```

```python
import functools
import math

import jax
import jax.numpy as jnp
from jax import lax
from jax.experimental import pallas as pl
from jax.experimental.pallas import tpu as pltpu
from jax.sharding import PartitionSpec as P

sharpness = 8.0
epsilon = 1e-06
base_weight = 8.0
MESH = pl.DeviceIdType.MESH
LOG2E = 1.4426950408889634
COLS = 2
QUAD = 2 * COLS
NEG = -1e30


def kernel(
    stages, chunks, detour, emb, ids, live, out,
    staged, e_sem, quad, vis, relay_rows, tags, tag_col, cap_col, acc, vsum, rsum, gpart, gsum,
    fwd_send, own_send, vis_recv, y_send, y_recv, i_send, i_recv, d_send, d_recv,
    x_recv, o_send, h_send, t_send, t_recv, r_send, r_recv, g_send, g_recv,
):
    rows, depth = emb.shape
    span = rows // chunks
    half = stages // 2 - 1
    blk, core = lax.axis_index("blk"), lax.axis_index("inner")
    odd = lax.axis_index("groups") % 2 if detour else 0
    group = lax.axis_index("groups")

    def flip(s):
        return s + odd * (stages - 1 - 2 * s)

    stage, col = flip(blk // COLS), blk % COLS
    upper = stage // (half + 1)
    q = col * 2 + core
    me = blk * 2 + core
    peers = stages * QUAD

    def at(s, y, c):
        return {"blk": flip(s) * COLS + y, "inner": c}

    def peer_of(index):
        return {"blk": index // 2, "inner": index % 2}

    def part(k):
        return pl.ds(pl.multiple_of(k * span, span), span)

    def remote(src, dst, send, recv, device):
        return pltpu.make_async_remote_copy(
            src_ref=src, dst_ref=dst, send_sem=send, recv_sem=recv,
            device_id=device, device_id_type=MESH,
        )

    def own_forward(k):
        return remote(quad.at[q, part(k)], vis.at[0, part(k)], own_send.at[k], vis_recv.at[0, k],
                      at(stage + 1, col, core))

    def own_back(k):
        return remote(quad.at[q, part(k)], vis.at[half + 1, part(k)], own_send.at[k],
                      vis_recv.at[half + 1, k], at(stage - 1, col, core))

    def pass_forward(s, k):
        slot = s + 1 - upper
        return remote(vis.at[s, part(k)], vis.at[slot, part(k)], fwd_send.at[s, k],
                      vis_recv.at[slot, k], at(stage + 1, col, core))

    def pass_back(s, k):
        slot = half + 1 + s
        return remote(vis.at[slot, part(k)], vis.at[slot + 1, part(k)], fwd_send.at[slot, k],
                      vis_recv.at[slot + 1, k], at(stage - 1, col, core))

    def arrival(slot, k):
        return remote(vis.at[slot, part(k)], vis.at[slot, part(k)], fwd_send.at[slot, k],
                      vis_recv.at[slot, k], at(stage, col, 1 - core))

    def across(owner, k):
        return remote(quad.at[owner, part(k)], quad.at[owner, part(k)], y_send.at[k], y_recv.at[k],
                      at(stage, 1 - col, core))

    def beside(owner, k):
        return remote(quad.at[owner, part(k)], quad.at[owner, part(k)], i_send.at[k], i_recv.at[k],
                      at(stage, col, 1 - core))

    def diagonal(owner, k):
        return remote(quad.at[owner, part(k)], quad.at[owner, part(k)], d_send.at[k], d_recv.at[k],
                      at(stage, col, 1 - core))

    twin = {"groups": group + 1 - 2 * odd}

    def relay_in(k):
        return remote(vis.at[0, part(k)], relay_rows.at[part(k)], fwd_send.at[0, k], x_recv.at[k], twin)

    def relay_on(k):
        return remote(relay_rows.at[part(k)], relay_rows.at[part(k)], o_send.at[k], x_recv.at[k],
                      at(stage - 1, col, core))

    def relay_home(k):
        return remote(relay_rows.at[part(k)], vis.at[1, part(k)], h_send.at[k], vis_recv.at[1, k], twin)

    def relay_arrival(k):
        return remote(relay_rows.at[part(k)], relay_rows.at[part(k)], o_send.at[k], x_recv.at[k], twin)

    def carry(k, role):
        if k < 0 or k >= detour:
            return

        @pl.when(stage == role)
        def _():
            relay_arrival(k).wait_recv()

            @pl.when(stage < 2)
            def _():
                relay_home(k).start()

            @pl.when(stage > 0)
            def _():
                relay_on(k).start()

    def tag_copy(owner, sem, device):
        return remote(tags.at[owner], tags.at[owner], t_send.at[sem], t_recv.at[owner], device)

    q_across, q_beside = (1 - col) * 2 + core, col * 2 + 1 - core
    q_diag = (1 - col) * 2 + 1 - core

    def load(k):
        return pltpu.make_async_copy(emb.at[part(k)], staged.at[part(k)], e_sem.at[k])

    for k in range(chunks):
        load(k).start()
    barrier = pltpu.get_barrier_semaphore()

    def greet(p, _):
        pl.semaphore_signal(barrier, inc=1, device_id=peer_of((me + p) % peers), device_id_type=MESH)
        return 0

    lax.fori_loop(1, peers, greet, 0)
    if detour:
        pl.semaphore_signal(barrier, inc=1, device_id=twin, device_id_type=MESH)

    def normalize(k):
        load(k).wait()
        wide = staged[part(k), :].astype(jnp.float32)
        scale = lax.rsqrt(jnp.mean(wide * wide, axis=1, keepdims=True) + epsilon) / math.sqrt(depth)
        quad[q, part(k), :] = (wide * scale).astype(jnp.bfloat16)

    position = lax.broadcasted_iota(jnp.int32, (1, rows), 1)
    tags[me] = jnp.where(position < live[0], ids[...], -1).astype(jnp.float32)
    normalize(0)
    pl.semaphore_wait(barrier, peers - 1 + (1 if detour else 0))

    def start_own(k):
        @pl.when(stage <= half)
        def _():
            own_forward(k).start()

        @pl.when(stage >= half + 2)
        def _():
            own_back(k).start()

        across(q, k).start()
        beside(q, k).start()

    def send_tags(p, _):
        tag_copy(me, p, peer_of((me + p) % peers)).start()
        return 0

    start_own(0)
    lax.fori_loop(1, peers, send_tags, 0)

    def rest(k, _):
        normalize(k)
        start_own(k)
        return 0

    lax.fori_loop(1, chunks, rest, 0)

    def receive(s, k):
        @pl.when(stage > s)
        def _():
            arrival(s, k).wait_recv()

            if s == 0 and k < detour:
                @pl.when(stage == 1)
                def _():
                    relay_in(k).start()

                @pl.when(stage == 2)
                def _():
                    pass_forward(s, k).start()
            elif s > 0 and k < detour:
                pass
            else:
                @pl.when(stage < stages - 1)
                def _():
                    pass_forward(s, k).start()

        if s <= stages - 3 - half:
            @pl.when((stage > half) & (stage + s < stages - 1))
            def _():
                arrival(half + 1 + s, k).wait_recv()

                @pl.when(stage >= half + 2)
                def _():
                    pass_back(s, k).start()

    def take_tags(p, _):
        tag_copy((me + p) % peers, p, peer_of((me + p) % peers)).wait_recv()
        return 0

    def lay_tags(g):
        row = tags[flip(stage) * QUAD + g]
        tall = jnp.broadcast_to(row, (128, rows)).T
        tag_col[g] = tall
        cap_col[g] = jnp.where(tall < 0, NEG, 0.0)
        acc[g] = jnp.zeros((rows, 128), jnp.float32)

    for k in range(chunks):
        if k == 2:
            lax.fori_loop(1, peers, take_tags, 0)
        if 2 <= k < 2 + QUAD:
            lay_tags(k - 2)
        receive(0, k)
        carry(k - 1, 2)
        carry(k - 2, 1)
        carry(k - 3, 0)
        across(q_across, k).wait_recv()
        diagonal(q_across, k).start()

    def settle(k, _):
        beside(q_beside, k).wait_recv()
        diagonal(q_diag, k).wait_recv()
        return 0

    lax.fori_loop(0, chunks, settle, 0)

    third = rows // 2 + rows // 4
    bounds = {0: (0, rows // 2), 1: (rows // 2, rows), 2: (rows // 2, third), 3: (third, rows)}

    def visit(block, owner, slot, u, keep):
        low, high = bounds[u]
        unit = high - low
        lanes = slice(low, high)
        seen = block[lanes, :]
        tag_row = tags[owner, :, lanes]
        same = jnp.where(tag_row < 0, NEG, -sharpness * LOG2E)
        other = same - 2.0
        total = jnp.zeros((8, unit), jnp.float32)
        tall = rows // 2
        for g in range(QUAD):
            for t in range(rows // tall):
                down = slice(t * tall, (t + 1) * tall)
                cosines = lax.dot_general(
                    quad[g, down, :], seen, (((1,), (1,)), ((), ())),
                    preferred_element_type=jnp.float32,
                )
                scaled = cosines * (sharpness * LOG2E)
                kept = acc[g, down, :] if keep else None
                sums = []
                for b in range(unit // 128):
                    wide = slice(b * 128, (b + 1) * 128)
                    bias = jnp.where(tag_col[g, down, :] == tag_row[:, wide], same[:, wide], other[:, wide])
                    weight = jnp.exp2(scaled[:, wide] + (bias + cap_col[g, down, :]))
                    if keep:
                        kept = kept + weight
                    sums.append(jnp.sum(weight.reshape(tall // 8, 8, 128), axis=0))
                if keep:
                    acc[g, down, :] = kept
                total = total + jnp.concatenate(sums, axis=1)
        vsum[slot, :, lanes] = jnp.sum(total, axis=0, keepdims=True)

    def owner_of(visitor):
        return flip(visitor) * QUAD + q

    def from_below(s):
        return (stage - 1) * (1 - upper) + half * upper - s

    def visit_forward(s, u):
        @pl.when(stage > s)
        def _():
            visit(vis.at[s], owner_of(from_below(s)), s, u, True)

    def visit_back(s, u):
        if s <= stages - 3 - half:
            @pl.when((stage > half) & (stage + s < stages - 1))
            def _():
                visit(vis.at[half + 1 + s], owner_of(stage + 1 + s), half + 1 + s, u, True)

    def visit_own(u):
        visit(quad.at[q], me, stages - 1, u, False)

    for k in range(chunks, chunks + 3):
        carry(k - 1, 2)
        carry(k - 2, 1)
        carry(k - 3, 0)
    visit_own(0)
    direct = list(range(detour, chunks)) if detour else []
    waiting = [k for k in range(chunks) if k not in direct]
    for k in direct[:1]:
        receive(1, k)
    visit_forward(0, 0)
    visit_back(0, 0)
    for k in direct[1:2]:
        receive(1, k)
    for k in waiting[:chunks // 2]:
        receive(1, k)
    visit_forward(1, 0)
    visit_back(1, 0)
    visit_own(1)
    visit_forward(0, 1)
    for k in direct[2:]:
        receive(1, k)
    visit_back(0, 1)
    for k in waiting[chunks // 2:]:
        if k < third // span:
            receive(1, k)
    visit_forward(1, 2)
    visit_back(1, 2)
    for k in waiting[chunks // 2:]:
        if k >= third // span:
            receive(1, k)
    visit_forward(1, 3)
    visit_back(1, 3)
    for s in range(2, half + 1):
        for u in range(2):
            for k in range(u * chunks // 2, (u + 1) * chunks // 2):
                receive(s, k)
            visit_forward(s, u)
            visit_back(s, u)

    def give_back(slot, visitor):
        return remote(vsum.at[slot], rsum.at[stage], r_send.at[slot], r_recv.at[stage],
                      at(visitor, col, core))

    def each_return(act):
        for s in range(half + 1):
            @pl.when(stage > s)
            def _():
                act(give_back(s, from_below(s)))

            if s <= stages - 3 - half:
                @pl.when((stage > half) & (stage + s < stages - 1))
                def _():
                    act(give_back(half + 1 + s, stage + 1 + s))

    each_return(lambda copy: copy.start())
    for g in range(QUAD):
        gpart[g] = jnp.sum(acc[g].T, axis=0, keepdims=True)

    def share(step):
        g = (q + step) % QUAD
        return remote(gpart.at[g], gsum.at[q], g_send.at[step], g_recv.at[q], at(stage, g // 2, g % 2))

    def shared(step):
        g = (q + step) % QUAD
        return remote(gpart.at[g], gsum.at[g], g_send.at[step], g_recv.at[g], at(stage, g // 2, g % 2))

    for step in range(1, QUAD):
        share(step).start()
    vsum[stages - 1] = vsum[stages - 1] + gpart[q]
    for other in range(stages):
        @pl.when(((stage <= half) & (other > stage)) | ((stage > other) & (other > half)))
        def _():
            remote(rsum.at[other], rsum.at[other], r_send.at[0], r_recv.at[other],
                   at(stage, col, 1 - core)).wait_recv()
            vsum[stages - 1] = vsum[stages - 1] + rsum[other]

    for step in range(1, QUAD):
        shared(step).wait_recv()
        vsum[stages - 1] = vsum[stages - 1] + gsum[(q + step) % QUAD]
    mask = (tags[me] >= 0).astype(jnp.float32)
    out[...] = mask * base_weight / (vsum[stages - 1] + 1.0 - mask)

    for k in range(chunks):
        @pl.when(stage <= half)
        def _():
            own_forward(k).wait_send()

        @pl.when(stage >= half + 2)
        def _():
            own_back(k).wait_send()

        across(q, k).wait_send()
        beside(q, k).wait_send()
        diagonal(q_across, k).wait_send()
        for s in range(half + 1):
            if s == 0 and k < detour:
                @pl.when((stage == 1) | (stage == 2))
                def _():
                    pass_forward(s, k).wait_send()
            elif s > 0 and k < detour:
                pass
            else:
                @pl.when((stage > s) & (stage < stages - 1))
                def _():
                    pass_forward(s, k).wait_send()

            if s <= stages - 3 - half:
                @pl.when((stage >= half + 2) & (stage + s < stages - 1))
                def _():
                    pass_back(s, k).wait_send()
        if k < detour:
            @pl.when(stage < 2)
            def _():
                relay_home(k).wait_send()

            @pl.when((stage > 0) & (stage < stages - 1))
            def _():
                relay_on(k).wait_send()

    def drain_tags(p, _):
        tag_copy(me, p, peer_of((me + p) % peers)).wait_send()
        return 0

    lax.fori_loop(1, peers, drain_tags, 0)
    each_return(lambda copy: copy.wait_send())
    for step in range(1, QUAD):
        share(step).wait_send()


def solution(mesh):
    stages = mesh.shape["blk"] // COLS

    def body(embeddings, cluster_ids, live_rows):
        rows, depth = embeddings.shape
        chunks = 8
        detour = 5 if stages == 4 and mesh.shape["groups"] % 2 == 0 else 0
        peers = stages * QUAD
        dma = pltpu.SemaphoreType.DMA
        f32 = jnp.float32
        weights = pl.pallas_call(
            functools.partial(kernel, stages, chunks, detour),
            out_shape=jax.ShapeDtypeStruct((1, rows), f32),
            in_specs=[
                pl.BlockSpec(memory_space=pl.ANY),
                pl.BlockSpec(memory_space=pltpu.VMEM),
                pl.BlockSpec(memory_space=pltpu.SMEM),
            ],
            out_specs=pl.BlockSpec(memory_space=pltpu.VMEM),
            scratch_shapes=[
                pltpu.VMEM((rows, depth), jnp.bfloat16),
                dma((chunks,)),
                pltpu.VMEM((QUAD, rows, depth), jnp.bfloat16),
                pltpu.VMEM((stages - 1, rows, depth), jnp.bfloat16),
                pltpu.VMEM((rows, depth), jnp.bfloat16),
                pltpu.VMEM((peers, 1, rows), f32),
                pltpu.VMEM((QUAD, rows, 128), f32),
                pltpu.VMEM((QUAD, rows, 128), f32),
                pltpu.VMEM((QUAD, rows, 128), f32),
                pltpu.VMEM((stages, 1, rows), f32),
                pltpu.VMEM((stages, 1, rows), f32),
                pltpu.VMEM((QUAD, 1, rows), f32),
                pltpu.VMEM((QUAD, 1, rows), f32),
                dma((stages - 1, chunks)),
                dma((chunks,)),
                dma((stages - 1, chunks)),
                dma((chunks,)), dma((chunks,)),
                dma((chunks,)), dma((chunks,)),
                dma((chunks,)), dma((chunks,)),
                dma((chunks,)), dma((chunks,)), dma((chunks,)),
                dma((peers,)), dma((peers,)),
                dma((stages - 1,)), dma((stages,)),
                dma((QUAD,)), dma((QUAD,)),
            ],
            compiler_params=pltpu.CompilerParams(
                collective_id=0, has_side_effects=True, vmem_limit_bytes=48 * 1024 * 1024
            ),
        )(embeddings, cluster_ids.reshape(1, rows), live_rows)
        return weights.reshape(rows)

    return jax.shard_map(
        body,
        mesh=mesh,
        in_specs=(
            P(("groups", "blk", "inner"), None),
            P(("groups", "blk", "inner")),
            P(("groups", "blk", "inner")),
        ),
        out_specs=P(("groups", "blk", "inner")),
        check_vma=False,
    )
```
